256 devices in a mesh: grp: 16 (over z, core), dp: 8 (over y, x_hi), head: 2 (over x_lo).
Axes of the slice: x: 4 (x_hi: 2, x_lo: 2; x = x_hi * 2 + x_lo), y: 4, z: 8, core: 2. Of those that a mesh axis runs over, the one named last changes fastest.
Arguments:
- queries: bfloat16 [16384, 4096], P(('dp', 'grp'), 'head'), parts along dimension 0, may hold values from -5 to 5
- out_grad: bfloat16 [16384, 4096], P(('dp', 'grp'), 'head'), parts along dimension 0, may hold values from -24 to 24
- resp_keys: bfloat16 [16384, 1024], P(('dp', 'grp'), 'head'), parts along dimension 0, may hold values from -10 to 10
- response_values: bfloat16 [16384, 1024], P(('dp', 'grp'), 'head'), parts along dimension 0, may hold values from -12 to 12
- prompt_keys: bfloat16 [16384, 1024], P(('dp', 'grp'), 'head'), parts along dimension 0, may hold values from -10 to 10
- prompt_value_rows: bfloat16 [16384, 1024], P(('dp', 'grp'), 'head'), parts along dimension 0, may hold values from -12 to 12
- lengths: int32 [128], P(('dp', 'grp')), parts along dimension 0, may hold values from 1 to 128, 1536 in all
- tree_mask: int32 [128, 16], P(('dp', 'grp')), parts along dimension 0, may hold values from 0 to 1, as said below
- prompt_order: int32 [128], P('dp'), parts along dimension 0, may hold values from 0 to 15, as said below
Outputs:
- query_gradient: float32 [16384, 4096], P(('dp', 'grp'), 'head'), parts along dimension 0
- response_key_gradient: float32 [16384, 1024], P(('dp', 'grp'), 'head'), parts along dimension 0
- response_value_gradient: float32 [16384, 1024], P(('dp', 'grp'), 'head'), parts along dimension 0
- prompt_keygrad: float32 [16384, 1024], P(('dp', 'grp'), 'head'), parts along dimension 0
- prompt_valgrad: float32 [16384, 1024], P(('dp', 'grp'), 'head'), parts along dimension 0
The draws below stay inside these ranges and needn't reach their ends.
There are 8 independent parts, one for each index of `dp`. The reference program is written for one: setup_inputs(seed, part) draws one part's arguments, and reference() takes and returns one part's arrays. A program takes and returns all parts, laid end to end along the dimension named above; each array names one. Nothing has to cross between parts.
Inputs may be any that keep to these rules, and one draw needn't show every extreme that they name: `tree_mask`: row g marks the tree tiles on the path from root tile 0 to one tile of a tree in which each tile's parent is an earlier tile; tile 0 is marked in every row and every tile is marked in some row. A permutation: prompt slot s (prompt tokens s * 128 to (s + 1) * 128 - 1) holds tree tile prompt_order[s]. `lengths`: some response has all 128 tokens live.
All inputs are finite; a program needn't handle non-finite values. No bound on the sum of `lengths` on one device may be relied on, other than what follows from the above.
Results may differ from the reference program's by a relative error of at most 0.0039.
Values may be sent and summed in bfloat16 or wider, within the bound.
A program may use at most 128 MiB of HBM per device.

```python
import math
import jax
import jax.numpy as jnp
import numpy as np
from jax import lax

HEAD_WIDTH = 128
QUERY_HEADS = 32
KEY_VALUE_HEADS = 8
TILE = 128
RESPONSE_SLOTS = 128
PROMPT_TOKENS = 2048
TOKEN_SLOTS = 2048
PTILES = 16
N_GRP = 16


def slot_order(key):
    return jax.random.permutation(jax.random.fold_in(key, 502), PTILES).astype(jnp.int32)


def draw_queries(key, part):
    key = jax.random.fold_in(key, 11)
    scale_key, value_random_key = jax.random.split(key)
    scale_per_row = jnp.exp(jax.random.uniform(scale_key, (TOKEN_SLOTS, 1), jnp.float32, math.log(0.5), math.log(1.5)))
    value_tensor = 0.6 * jnp.clip(jax.random.normal(value_random_key, (TOKEN_SLOTS, QUERY_HEADS * HEAD_WIDTH), jnp.float32), -4.0, 4.0) * scale_per_row
    return value_tensor.astype(jnp.bfloat16)


def draw_resp_keys(key, part):
    key = jax.random.fold_in(key, 17)
    scale_key, value_random_key = jax.random.split(key)
    scale_per_row = jnp.exp(jax.random.uniform(scale_key, (TOKEN_SLOTS, 1), jnp.float32, math.log(0.25), math.log(2.5)))
    value_tensor = jnp.clip(jax.random.normal(value_random_key, (TOKEN_SLOTS, KEY_VALUE_HEADS * HEAD_WIDTH), jnp.float32), -4.0, 4.0) * scale_per_row
    return value_tensor.astype(jnp.bfloat16)


def draw_prompt_keys(key, part):
    key = jax.random.fold_in(key, 13)
    scale_key, value_random_key = jax.random.split(key)
    scale_per_row = jnp.exp(jax.random.uniform(scale_key, (PROMPT_TOKENS, 1), jnp.float32, math.log(0.25), math.log(2.5)))
    value_tensor = jnp.clip(jax.random.normal(value_random_key, (PROMPT_TOKENS, KEY_VALUE_HEADS * HEAD_WIDTH), jnp.float32), -4.0, 4.0) * scale_per_row
    return value_tensor.astype(jnp.bfloat16)


def draw_prompt_order(key, part):
    shared_order = slot_order(key)
    return shared_order


def draw_tree_mask(key, part):
    key = jax.random.fold_in(key, 19)
    chain_key, jump_key, perm_key, extra_key = jax.random.split(key, 4)
    tile_ids = jnp.arange(PTILES)
    chained = jax.random.randint(chain_key, (PTILES,), 0, 2)
    jumped = jax.random.randint(jump_key, (PTILES,), 0, jnp.maximum(tile_ids, 1))
    parent = jnp.where(chained == 1, jnp.maximum(tile_ids - 1, 0), jumped)
    shuffled = jax.random.permutation(perm_key, PTILES)
    others = jax.random.randint(extra_key, (N_GRP,), 0, PTILES)
    members = jnp.arange(N_GRP)
    leaf_tile = jnp.where(members < PTILES, shuffled[members % PTILES], others)

    def climb(turn_id, carried):
        marked, current = carried
        current = parent[current]
        return (marked | (current[:, None] == tile_ids[None, :]), current)
    start_marks = leaf_tile[:, None] == tile_ids[None, :]
    marked, final_tile = lax.fori_loop(0, PTILES, climb, (start_marks, leaf_tile))
    return marked.astype(jnp.int32)


def block_levels(key, extent, cuts, smallest, largest):
    loudness = 1.0
    for dim, shards_of in cuts:
        steps = jax.random.uniform(jax.random.fold_in(jax.random.fold_in(key, 6), dim), (shards_of,), jnp.float32, smallest / len(cuts), largest / len(cuts))
        loudness = loudness * jnp.repeat(jnp.exp(steps), extent[dim] // shards_of).reshape((-1,) + (1,) * (len(extent) - 1 - dim))
    return loudness


def length_profile(number_of, total, reach, lean):
    loads = [(1 << 20) // math.isqrt(standing ** lean) + 1 for standing in range(2, number_of + 1)]
    spare, given = total - reach - (number_of - 1), [1] * (number_of - 1)
    while spare > 0:
        movable = [i for i in range(number_of - 1) if given[i] < reach]
        pool, budget = sum([loads[i] for i in movable]), spare
        for i in movable:
            more = min(reach - given[i], max(1, budget * loads[i] // pool), spare)
            given[i] = given[i] + more
            spare = spare - more
    return np.array([reach] + given)


def uneven_parts(rng, count, total, most, slope):
    if count == 2:
        one = jax.random.randint(rng, (), max(1, total - most), min(most, total - 1) + 1)
        return jnp.stack([one, total - one])
    sizes = jnp.asarray(length_profile(count, total, most, slope), jnp.int32)
    twos = (count - 1) // 2
    donor, receiver = sizes[1:1 + 2 * twos:2], sizes[2:2 + 2 * twos:2]
    room = jnp.minimum(donor - 1, most - receiver)
    moved = jax.random.randint(jax.random.fold_in(rng, 1), (twos,), 0, 1 << 20) % (room + 1)
    sizes = sizes.at[1:1 + 2 * twos:2].set(donor - moved).at[2:2 + 2 * twos:2].set(receiver + moved)
    return sizes[jax.random.permutation(jax.random.fold_in(rng, 2), count)]


def centred(key, shape, scale, bound, cuts=(), dtype=jnp.bfloat16):
    factor_of = block_levels(key, shape, cuts, -0.22, 0.18) if cuts else 1.0
    drawn = jax.random.normal(key, shape, jnp.float32) * scale * factor_of
    return jnp.minimum(jnp.maximum(drawn, -bound), bound).astype(dtype)


def setup_inputs(seed: int = 0, part: int = 0) -> dict:
    key_of = jax.random.split(jax.random.key(seed), 10)
    part_keys = jax.random.split(jax.random.fold_in(key_of[9], part), 10)
    queries = draw_queries(jax.random.fold_in(jax.random.fold_in(key_of[9], part), 71), part)
    out_grad = centred(part_keys[1], (TOKEN_SLOTS, QUERY_HEADS * HEAD_WIDTH), 4.0, 24.0, ((0, 16), (1, 2)))
    resp_keys = draw_resp_keys(jax.random.fold_in(jax.random.fold_in(key_of[9], part), 71), part)
    response_values = centred(part_keys[3], (TOKEN_SLOTS, KEY_VALUE_HEADS * HEAD_WIDTH), 2.0, 12.0, ((0, 16), (1, 2)))
    prompt_keys = draw_prompt_keys(jax.random.fold_in(jax.random.fold_in(key_of[9], part), 71), part)
    prompt_value_rows = centred(part_keys[5], (PROMPT_TOKENS, KEY_VALUE_HEADS * HEAD_WIDTH), 2.0, 12.0, ((0, 16), (1, 2)))
    lengths = uneven_parts(part_keys[6], N_GRP, 3 * N_GRP * RESPONSE_SLOTS // 4, RESPONSE_SLOTS, 1).astype(jnp.int32)
    tree_mask = draw_tree_mask(jax.random.fold_in(jax.random.fold_in(key_of[9], part), 71), part)
    prompt_order = draw_prompt_order(jax.random.fold_in(jax.random.fold_in(key_of[9], part), 71), part)
    return {"queries": queries, "out_grad": out_grad, "resp_keys": resp_keys, "response_values": response_values, "prompt_keys": prompt_keys, "prompt_value_rows": prompt_value_rows, "lengths": lengths, "tree_mask": tree_mask, "prompt_order": prompt_order}


masked_fill = -1e+30

def einsum_wide(form, left, right):
    return jnp.einsum(form, left.astype(jnp.float32), right.astype(jnp.float32), precision=lax.Precision.HIGHEST)

def response_grads(rows_of_queries, gradient_rows, rows_of_keys, rows_of_values, length, visible):
    group_members = QUERY_HEADS // KEY_VALUE_HEADS
    inv_root = 1.0 / math.sqrt(HEAD_WIDTH)
    query_halves = rows_of_queries.reshape(RESPONSE_SLOTS, KEY_VALUE_HEADS, group_members, HEAD_WIDTH)
    gradient_split = gradient_rows.reshape(RESPONSE_SLOTS, KEY_VALUE_HEADS, group_members, HEAD_WIDTH)
    head_keys = rows_of_keys.reshape(-1, KEY_VALUE_HEADS, HEAD_WIDTH)
    head_values = rows_of_values.reshape(-1, KEY_VALUE_HEADS, HEAD_WIDTH)
    position = jnp.arange(RESPONSE_SLOTS)
    causal = position[None, :] <= position[:, None]
    prompt_part = jnp.broadcast_to(visible[None, :], (RESPONSE_SLOTS, PROMPT_TOKENS))
    allowed = jnp.concatenate([prompt_part, causal], axis=1)
    scores = einsum_wide('rkgd,lkd->kgrl', query_halves, head_keys) * inv_root
    grad_dot = einsum_wide('rkgd,lkd->kgrl', gradient_split, head_values)
    masked = jnp.where(allowed, scores, masked_fill)
    row_max = lax.optimization_barrier(jnp.max(masked, axis=-1, keepdims=True))
    shifted = jnp.exp(jnp.where(allowed, scores - row_max, masked_fill))
    exp_total = lax.optimization_barrier(jnp.sum(shifted, axis=-1))
    log_total = row_max[..., 0] + jnp.log(exp_total)
    row_delta = lax.optimization_barrier(jnp.sum(shifted * grad_dot, axis=-1)) / exp_total
    live = allowed & (position < length)[:, None]
    attn_prob = jnp.exp(jnp.where(live, scores - log_total[..., None], masked_fill))
    prob_half = attn_prob.astype(jnp.bfloat16)
    dscore = (attn_prob * (grad_dot - row_delta[..., None])).astype(jnp.bfloat16)
    response_value_gradient = einsum_wide('kgrl,rkgd->lkd', prob_half, gradient_split)
    query_gradient = einsum_wide('kgrl,lkd->rkgd', dscore, head_keys) * inv_root
    response_key_gradient = einsum_wide('kgrl,rkgd->lkd', dscore, query_halves) * inv_root
    key_total_count = response_key_gradient.shape[0]
    return (query_gradient.reshape(RESPONSE_SLOTS, QUERY_HEADS * HEAD_WIDTH), response_key_gradient.reshape(key_total_count, KEY_VALUE_HEADS * HEAD_WIDTH), response_value_gradient.reshape(key_total_count, KEY_VALUE_HEADS * HEAD_WIDTH))

def reference(queries, out_grad, resp_keys, response_values, prompt_keys, prompt_value_rows, lengths, tree_mask, prompt_order):
    tile_of = prompt_order[jnp.arange(PROMPT_TOKENS) // TILE]
    seen = tree_mask[:, tile_of] > 0
    query_width = QUERY_HEADS * HEAD_WIDTH
    paired_width = KEY_VALUE_HEADS * HEAD_WIDTH
    query_groups = queries.reshape(N_GRP, RESPONSE_SLOTS, query_width)
    grad_groups = out_grad.reshape(N_GRP, RESPONSE_SLOTS, query_width)
    key_groups = resp_keys.reshape(N_GRP, RESPONSE_SLOTS, paired_width)
    value_groups = response_values.reshape(N_GRP, RESPONSE_SLOTS, paired_width)

    def one_response(running, inputs):
        rows_of_queries, gradient_rows, own_keys, own_values, length, visible = inputs
        rows_of_keys = jnp.concatenate([prompt_keys, own_keys], axis=0)
        rows_of_values = jnp.concatenate([prompt_value_rows, own_values], axis=0)
        query_part, key_part, value_part = response_grads(rows_of_queries, gradient_rows, rows_of_keys, rows_of_values, length, visible)
        updated = (running[0] + key_part[:PROMPT_TOKENS], running[1] + value_part[:PROMPT_TOKENS])
        return (updated, (query_part, key_part[PROMPT_TOKENS:], value_part[PROMPT_TOKENS:]))
    initial = (jnp.zeros((PROMPT_TOKENS, paired_width), jnp.float32), jnp.zeros((PROMPT_TOKENS, paired_width), jnp.float32))
    sums, stacked = lax.scan(one_response, initial, (query_groups, grad_groups, key_groups, value_groups, lengths, seen))
    return (stacked[0].reshape(TOKEN_SLOTS, query_width), stacked[1].reshape(TOKEN_SLOTS, paired_width), stacked[2].reshape(TOKEN_SLOTS, paired_width), sums[0], sums[1])
```

```python
import functools
import math

import jax
import jax.numpy as jnp
from jax import lax
from jax.experimental import pallas as pl
from jax.experimental.pallas import tpu as pltpu
from jax.sharding import PartitionSpec as P

MESH = pl.DeviceIdType.MESH
WIDTH = 128
RING = 8
HEADS = 2
MEMBERS = 4
HALF = MEMBERS * WIDTH
ROWS = 2 * HALF
CHUNK = 2 * WIDTH
LANES = 256
UP, DOWN = 0, 1
KEY, VALUE = 0, 1
HOPS = ((4, 3), (3, 4))
ROOT = 1.0 / math.sqrt(WIDTH)
SCALE = ROOT * math.log2(math.e)
HIDDEN = -1e30


def dot_nt(a, b):
    return lax.dot_general(a, b, (((1,), (1,)), ((), ())), preferred_element_type=jnp.float32)


def dot_nn(a, b):
    return jnp.dot(a, b, preferred_element_type=jnp.float32)


def dot_tn(a, b):
    return lax.dot_general(a, b, (((0,), (0,)), ((), ())), preferred_element_type=jnp.float32)


def slot_of(direction, hop):
    return hop if direction == UP else RING - hop


def kernel(
    q_ref, og_ref, rk_ref, rv_ref, pk_ref, pv_ref, len_ref, mask_ref, order_ref,
    dq_out, drk_out, drv_out, dpk_out, dpv_out,
    qin, oin, rkin, rvin, meta, qs, os_, kv,
    e_buf, d_buf, er_buf, dr_buf, m_run, l_run, w_run, m_save, mr_save, p_tmp, ds_buf, dsr_buf,
    grad, sbuf, rbuf, fin, mate_grad, dq_t, dq_stage, drk_stage, drv_stage,
    loc_sem, pair_send, pair_recv, ag_send, ag_recv, rs_send, rs_recv,
):
    me = lax.axis_index("grp")
    z, c = me // 2, me % 2
    other = 1 - c
    above, below = (z + 1) % RING, (z + RING - 1) % RING
    straight = (above * 2 + c, below * 2 + c)
    cross = (above * 2 + other, below * 2 + other)
    mate = z * 2 + other

    def remote(src, dst, send, recv, target):
        return pltpu.make_async_remote_copy(
            src_ref=src, dst_ref=dst, send_sem=send, recv_sem=recv,
            device_id={"grp": target}, device_id_type=MESH,
        )

    def cols(core, width, start=0, size=None):
        size = width if size is None else size
        return pl.ds(pl.multiple_of(core * width + start, WIDTH), size)

    def half(core):
        return pl.ds(pl.multiple_of(core * WIDTH, WIDTH), WIDTH)

    prompt = (pk_ref, pv_ref)

    local = [
        pltpu.make_async_copy(q_ref.at[:, cols(c, 1024)], qin.at[0], loc_sem.at[0]),
        pltpu.make_async_copy(og_ref.at[:, cols(c, 1024)], oin.at[0], loc_sem.at[1]),
        pltpu.make_async_copy(rk_ref.at[:, cols(c, 256)], rkin.at[0], loc_sem.at[2]),
        pltpu.make_async_copy(rv_ref.at[:, cols(c, 256)], rvin.at[0], loc_sem.at[3]),
    ]
    for t in range(2):
        for hh in range(HEADS):
            local.append(
                pltpu.make_async_copy(
                    prompt[t].at[:, cols(c, 256, hh * WIDTH, WIDTH)],
                    kv.at[t, hh, 0, half(c)],
                    loc_sem.at[4 + t * HEADS + hh],
                )
            )
    for copy in local:
        copy.start()

    for s in range(16):
        seen = mask_ref[0, order_ref[s]]
        row = jnp.full((1, LANES), seen, jnp.int32).astype(jnp.float32)
        meta[0, pl.ds(s, 1), :] = (1.0 - jnp.minimum(row, 1.0)) * HIDDEN
    meta[0, pl.ds(16, 8), :] = jnp.full((8, LANES), len_ref[0], jnp.int32).astype(jnp.float32)

    barrier = pltpu.get_barrier_semaphore()
    for target in (*straight, *cross, mate):
        pl.semaphore_signal(barrier, inc=1, device_id={"grp": target}, device_id_type=MESH)
    pl.semaphore_wait(barrier, 5)

    sends = []

    def start(copy):
        copy.start()
        sends.append(copy)
        return copy

    def first_hop(hh):
        for t in range(2):
            for d in (UP, DOWN):
                slot = slot_of(d, 1)
                for way, (core, target) in enumerate(((c, straight[d]), (other, cross[d]))):
                    start(
                        remote(
                            prompt[t].at[:, cols(core, 256, hh * WIDTH, WIDTH)],
                            kv.at[t, hh, slot, half(c)],
                            ag_send.at[t, hh, d, way],
                            ag_recv.at[t, hh, d, way],
                            target,
                        )
                    )

    def pair(i, src, dst):
        return start(remote(src, dst, pair_send.at[i], pair_recv.at[i], mate))

    first_hop(0)
    pair_copies = [
        pair(0, rk_ref.at[:, cols(other, 256)], rkin.at[1]),
        pair(1, rv_ref.at[:, cols(other, 256)], rvin.at[1]),
        pair(2, meta.at[0], meta.at[1]),
        pair(3, q_ref.at[:, cols(other, 1024)], qin.at[1]),
        pair(4, og_ref.at[:, cols(other, 1024)], oin.at[1]),
    ]
    for t in range(2):
        for hh in range(HEADS):
            pair_copies.append(
                pair(
                    5 + t * HEADS + hh,
                    prompt[t].at[:, cols(other, 256, hh * WIDTH, WIDTH)],
                    kv.at[t, hh, 0, half(c)],
                )
            )
    first_hop(1)

    for copy in local:
        copy.wait()
    for i, copy in enumerate(pair_copies[:5]):
        copy.wait_recv()

    for hh in range(HEADS):
        for p in range(2):
            for g in range(MEMBERS):
                rows = pl.ds(p * HALF + g * WIDTH, WIDTH)
                lanes = pl.ds((hh * MEMBERS + g) * WIDTH, WIDTH)
                qs[hh, rows, :] = qin[p, :, lanes]
                os_[hh, rows, :] = oin[p, :, lanes]

    def own_block(hh):
        for p in range(2):
            keys = rkin[p, :, pl.ds(hh * WIDTH, WIDTH)]
            values = rvin[p, :, pl.ds(hh * WIDTH, WIDTH)]

            @pl.loop(0, HALF // LANES)
            def _(b):
                lanes = pl.ds(pl.multiple_of(b * LANES, LANES), LANES)
                rows = pl.ds(pl.multiple_of(p * HALF + b * LANES, LANES), LANES)
                s = dot_nt(keys, qs[hh, rows, :])
                dp = dot_nt(values, os_[hh, rows, :])
                key_at = lax.broadcasted_iota(jnp.int32, (WIDTH, LANES), 0)
                row_at = lax.broadcasted_iota(jnp.int32, (WIDTH, LANES), 1) % WIDTH
                s = jnp.where(key_at <= row_at, s * SCALE, HIDDEN)
                top = jnp.max(s, axis=0, keepdims=True)
                e = jnp.exp2(s - top)
                er_buf[hh, p, :, lanes] = e
                dr_buf[hh, p, :, lanes] = dp
                m_run[hh, :, rows] = top
                mr_save[hh, :, rows] = top
                l_run[hh, :, rows] = jnp.sum(e, axis=0, keepdims=True)
                w_run[hh, :, rows] = jnp.sum(e * dp, axis=0, keepdims=True)

    def tile_bias(p, slot, part):
        tile = ((z + RING - slot) % RING) * 2 + part
        return meta[p, pl.ds(tile, 1), :]

    def forward(hh, slot):
        for p in range(2):
            bias = [tile_bias(p, slot, part) for part in range(2)]

            @pl.loop(0, HALF // LANES)
            def _(b):
                lanes = pl.ds(pl.multiple_of(p * HALF + b * LANES, LANES), LANES)
                s = dot_nt(kv[KEY, hh, slot], qs[hh, lanes, :])
                dp = dot_nt(kv[VALUE, hh, slot], os_[hh, lanes, :])
                d_buf[hh, slot, :, lanes] = dp
                old = m_run[hh, :, lanes]
                top = old
                for part in range(2):
                    high = jnp.max(s[part * WIDTH : (part + 1) * WIDTH], axis=0, keepdims=True)
                    top = jnp.maximum(top, high * SCALE + bias[part])
                less = jnp.exp2(old - top)
                total = l_run[hh, :, lanes] * less
                weighted = w_run[hh, :, lanes] * less
                for part in range(2):
                    rows = slice(part * WIDTH, (part + 1) * WIDTH)
                    e = jnp.exp2(s[rows] * SCALE - (top - bias[part]))
                    e_buf[hh, slot, rows, lanes] = e
                    total = total + jnp.sum(e, axis=0, keepdims=True)
                    weighted = weighted + jnp.sum(e * dp[rows], axis=0, keepdims=True)
                m_run[hh, :, lanes] = top
                m_save[hh, slot, :, lanes] = top
                l_run[hh, :, lanes] = total
                w_run[hh, :, lanes] = weighted

    own_block(0)
    own_block(1)
    for copy in pair_copies[5:]:
        copy.wait_recv()
    forward(0, 0)
    forward(1, 0)

    for hop in range(1, 5):
        for hh in range(HEADS):
            for t in range(2):
                for d in (UP, DOWN):
                    if hop > HOPS[t][d]:
                        continue
                    slot = slot_of(d, hop)
                    here = kv.at[t, hh, slot]
                    if hop == 1:
                        for way, core in enumerate((c, other)):
                            part = kv.at[t, hh, slot, half(core)]
                            remote(
                                part, part, ag_send.at[t, hh, d, way], ag_recv.at[t, hh, d, way], straight[d]
                            ).wait_recv()
                    else:
                        remote(
                            here, here, ag_send.at[t, hh, d, hop], ag_recv.at[t, hh, d, hop], straight[d]
                        ).wait_recv()
                    if hop < HOPS[t][d]:
                        start(
                            remote(
                                here,
                                kv.at[t, hh, slot_of(d, hop + 1)],
                                ag_send.at[t, hh, d, hop + 1],
                                ag_recv.at[t, hh, d, hop + 1],
                                straight[d],
                            )
                        )
            forward(hh, hop)
            if hop < 4:
                forward(hh, RING - hop)

    for hh in range(HEADS):
        for p in range(2):
            for b in range(HALF // LANES):
                lanes = pl.ds(p * HALF + b * LANES, LANES)
                total = l_run[hh, :, lanes]
                w_run[hh, :, lanes] = w_run[hh, :, lanes] / total
                at = (lax.broadcasted_iota(jnp.int32, (1, LANES), 1) % WIDTH).astype(jnp.float32)
                live = at < meta[p, pl.ds(16, 1), :]
                l_run[hh, :, lanes] = jnp.where(live, 1.0 / total, 0.0)

    def backward(hh, slot, keep):
        @pl.loop(0, ROWS // LANES)
        def _(b):
            lanes = pl.ds(pl.multiple_of(b * LANES, LANES), LANES)
            factor = jnp.exp2(m_save[hh, slot, :, lanes] - m_run[hh, :, lanes]) * l_run[hh, :, lanes]
            prob = e_buf[hh, slot, :, lanes] * factor
            p_tmp[:, lanes] = prob.astype(jnp.bfloat16)
            ds = prob * (d_buf[hh, slot, :, lanes] - w_run[hh, :, lanes])
            ds_buf[hh, slot, :, lanes] = ds.astype(jnp.bfloat16)

        grad[KEY, hh, keep] = dot_nn(ds_buf[hh, slot], qs[hh])
        grad[VALUE, hh, keep] = dot_nn(p_tmp[...], os_[hh])

    def pass_on(t, hh, d, hop, keep):
        i = hop - 1
        if hop == 1:
            sbuf[t, hh, d, i] = grad[t, hh, keep].astype(jnp.bfloat16)
        else:
            arrived = rbuf.at[t, hh, d, i - 1]
            remote(
                arrived, arrived, rs_send.at[t, hh, d, i - 1], rs_recv.at[t, hh, d, i - 1], straight[d]
            ).wait_recv()
            sbuf[t, hh, d, i] = (grad[t, hh, keep] + arrived[...].astype(jnp.float32)).astype(jnp.bfloat16)
        if hop < HOPS[t][d]:
            start(
                remote(
                    sbuf.at[t, hh, d, i],
                    rbuf.at[t, hh, d, i],
                    rs_send.at[t, hh, d, i],
                    rs_recv.at[t, hh, d, i],
                    straight[d],
                )
            )
        else:
            for way, (core, target) in enumerate(((c, straight[d]), (other, cross[d]))):
                start(
                    remote(
                        sbuf.at[t, hh, d, i, half(core)],
                        fin.at[t, hh, d, way],
                        rs_send.at[t, hh, d, 3 + way],
                        rs_recv.at[t, hh, d, 3 + way],
                        target,
                    )
                )

    for hh in range(HEADS):
        backward(hh, 4, 0)
        pass_on(KEY, hh, UP, 1, 0)
        pass_on(VALUE, hh, DOWN, 1, 0)
    for away in (3, 2, 1):
        for hh in range(HEADS):
            backward(hh, RING - away, 0)
            backward(hh, away, 1)
            for t in ((VALUE, KEY) if away == 3 else (KEY, VALUE)):
                pass_on(t, hh, UP, HOPS[t][UP] - away + 1, 0)
            for t in (KEY, VALUE):
                pass_on(t, hh, DOWN, HOPS[t][DOWN] - away + 1, 1)

    mates = []
    for hh in range(HEADS):
        backward(hh, 0, 0)
        for t in range(2):
            mates.append(pair(9 + t * HEADS + hh, grad.at[t, hh, 0, half(other)], mate_grad.at[t, hh]))

    for hh in range(HEADS):
        lanes = pl.ds(hh * WIDTH, WIDTH)
        for p in range(2):
            rows = pl.ds(p * HALF, HALF)
            factor = jnp.exp2(mr_save[hh, :, rows] - m_run[hh, :, rows]) * l_run[hh, :, rows]
            prob = er_buf[hh, p] * factor
            ds = (prob * (dr_buf[hh, p] - w_run[hh, :, rows])).astype(jnp.bfloat16)
            dsr_buf[hh, p] = ds
            drk_stage[p, :, lanes] = dot_nn(ds, qs[hh, rows, :]) * ROOT
            drv_stage[p, :, lanes] = dot_nn(prob.astype(jnp.bfloat16), os_[hh, rows, :])
    outs = [
        pltpu.make_async_copy(drk_stage.at[0], drk_out.at[:, cols(c, 256)], loc_sem.at[0]),
        pltpu.make_async_copy(drv_stage.at[0], drv_out.at[:, cols(c, 256)], loc_sem.at[1]),
    ]
    for copy in outs:
        copy.start()
    mates.append(pair(13, drk_stage.at[1], drk_out.at[:, cols(c, 256)]))
    mates.append(pair(14, drv_stage.at[1], drv_out.at[:, cols(c, 256)]))

    for hh in range(HEADS):
        for p in range(2):
            for b in range(HALF // LANES):
                lanes = pl.ds(p * HALF + b * LANES, LANES)
                dq_t[...] = dot_tn(
                    rkin[p, :, pl.ds(hh * WIDTH, WIDTH)], dsr_buf[hh, p, :, pl.ds(b * LANES, LANES)]
                )

                @pl.loop(0, RING)
                def _(slot):
                    dq_t[...] += dot_tn(kv[KEY, hh, slot], ds_buf[hh, slot, :, lanes])

                for i in range(LANES // WIDTH):
                    g = hh * MEMBERS + b * (LANES // WIDTH) + i
                    block = dq_t[:, pl.ds(i * WIDTH, WIDTH)]
                    dq_stage[p, :, pl.ds(g * WIDTH, WIDTH)] = block.T * ROOT
    copy = pltpu.make_async_copy(dq_stage.at[0], dq_out.at[:, cols(c, 1024)], loc_sem.at[2])
    copy.start()
    outs.append(copy)
    mates.append(pair(15, dq_stage.at[1], dq_out.at[:, cols(c, 1024)]))

    for copy in mates[:4]:
        copy.wait_recv()
    result = (dpk_out, dpv_out)
    for hh in range(HEADS):
        for t in range(2):
            for way, core in enumerate((c, other)):
                share = grad[t, hh, 0, half(c), :] if way == 0 else mate_grad[t, hh]
                for d in (UP, DOWN):
                    arrived = fin.at[t, hh, d, way]
                    remote(
                        arrived, arrived, rs_send.at[t, hh, d, 3 + way], rs_recv.at[t, hh, d, 3 + way], straight[d]
                    ).wait_recv()
                    share = share + arrived[...].astype(jnp.float32)
                if t == KEY:
                    share = share * ROOT
                result[t][:, cols(core, 256, hh * WIDTH, WIDTH)] = share

    for copy in mates[4:]:
        copy.wait_recv()
    for copy in outs:
        copy.wait()
    for copy in sends:
        copy.wait_send()


def local(*args):
    bf16, f32 = jnp.bfloat16, jnp.float32
    vmem = pltpu.VMEM
    dma = pltpu.SemaphoreType.DMA
    any_ = pl.BlockSpec(memory_space=pl.ANY)
    smem = pl.BlockSpec(memory_space=pltpu.SMEM)
    in_vmem = pl.BlockSpec(memory_space=pltpu.VMEM)
    return pl.pallas_call(
        kernel,
        out_shape=(
            jax.ShapeDtypeStruct((WIDTH, 2048), f32),
            *(jax.ShapeDtypeStruct((WIDTH, 512), f32) for _ in range(4)),
        ),
        in_specs=[any_] * 6 + [smem] * 3,
        out_specs=(any_, any_, any_, in_vmem, in_vmem),
        scratch_shapes=[
            vmem((2, WIDTH, 1024), bf16),
            vmem((2, WIDTH, 1024), bf16),
            vmem((2, WIDTH, 256), bf16),
            vmem((2, WIDTH, 256), bf16),
            vmem((2, 24, LANES), f32),
            vmem((HEADS, ROWS, WIDTH), bf16),
            vmem((HEADS, ROWS, WIDTH), bf16),
            vmem((2, HEADS, RING, CHUNK, WIDTH), bf16),
            vmem((HEADS, RING, CHUNK, ROWS), f32),
            vmem((HEADS, RING, CHUNK, ROWS), f32),
            vmem((HEADS, 2, WIDTH, HALF), f32),
            vmem((HEADS, 2, WIDTH, HALF), f32),
            vmem((HEADS, 1, ROWS), f32),
            vmem((HEADS, 1, ROWS), f32),
            vmem((HEADS, 1, ROWS), f32),
            vmem((HEADS, RING, 1, ROWS), f32),
            vmem((HEADS, 1, ROWS), f32),
            vmem((CHUNK, ROWS), bf16),
            vmem((HEADS, RING, CHUNK, ROWS), bf16),
            vmem((HEADS, 2, WIDTH, HALF), bf16),
            vmem((2, HEADS, 2, CHUNK, WIDTH), f32),
            vmem((2, HEADS, 2, 4, CHUNK, WIDTH), bf16),
            vmem((2, HEADS, 2, 3, CHUNK, WIDTH), bf16),
            vmem((2, HEADS, 2, 2, WIDTH, WIDTH), bf16),
            vmem((2, HEADS, WIDTH, WIDTH), f32),
            vmem((WIDTH, LANES), f32),
            vmem((2, WIDTH, 1024), f32),
            vmem((2, WIDTH, 256), f32),
            vmem((2, WIDTH, 256), f32),
            dma((8,)),
            dma((16,)),
            dma((16,)),
            dma((2, HEADS, 2, 5)),
            dma((2, HEADS, 2, 5)),
            dma((2, HEADS, 2, 5)),
            dma((2, HEADS, 2, 5)),
        ],
        compiler_params=pltpu.CompilerParams(
            collective_id=0, has_side_effects=True, vmem_limit_bytes=60 * 1024 * 1024
        ),
        name="tree_attention_backward",
    )(*args)


def solution(mesh):
    rows = P(("dp", "grp"), "head")
    return jax.shard_map(
        local,
        mesh=mesh,
        in_specs=(rows,) * 6 + (P(("dp", "grp")), P(("dp", "grp"), None), P("dp")),
        out_specs=(rows,) * 5,
        check_vma=False,
    )
```

```python
import functools
import math

import jax
import jax.numpy as jnp
from jax import lax
from jax.experimental import pallas as pl
from jax.experimental.pallas import tpu as pltpu
from jax.sharding import PartitionSpec as P

MESH = pl.DeviceIdType.MESH
WIDTH = 128
RING = 8
HEADS = 2
MEMBERS = 4
HALF = MEMBERS * WIDTH
ROWS = 2 * HALF
CHUNK = 2 * WIDTH
LANES = 512
UP, DOWN = 0, 1
KEY, VALUE = 0, 1
HOPS = ((4, 3), (3, 4))
ROOT = 1.0 / math.sqrt(WIDTH)
SCALE = ROOT * math.log2(math.e)
HIDDEN = -1e30
MIB = 1024 * 1024


def dot_nt(a, b):
    return lax.dot_general(a, b, (((1,), (1,)), ((), ())), preferred_element_type=jnp.float32)


def dot_nn(a, b):
    return jnp.dot(a, b, preferred_element_type=jnp.float32)


def dot_tn(a, b):
    return lax.dot_general(a, b, (((0,), (0,)), ((), ())), preferred_element_type=jnp.float32)


def slot_of(direction, hop):
    return hop if direction == UP else RING - hop


def kernel(
    q_ref, og_ref, rk_ref, rv_ref, pk_ref, pv_ref, len_ref, mask_ref, order_ref,
    dq_out, drk_out, drv_out, dpk_out, dpv_out,
    qin, oin, rkin, rvin, meta, qs, os_, kv,
    e_buf, d_buf, er_buf, dr_buf, m_run, l_run, w_run, m_save, mr_save, p_tmp, ds_tmp,
    grad, sbuf, rbuf, fin, mate_grad, dq_t, dq_stage, drk_stage, drv_stage,
    loc_sem, send_sem, pair_recv, ag_recv, rs_recv,
):
    me = lax.axis_index("grp")
    z, c = me // 2, me % 2
    other = 1 - c
    above, below = (z + 1) % RING, (z + RING - 1) % RING
    straight = (above * 2 + c, below * 2 + c)
    cross = (above * 2 + other, below * 2 + other)
    mate = z * 2 + other
    mine = c
    theirs = 1 - mine

    def remote(src, dst, send, recv, target):
        return pltpu.make_async_remote_copy(
            src_ref=src, dst_ref=dst, send_sem=send, recv_sem=recv,
            device_id={"grp": target}, device_id_type=MESH,
        )

    def cols(core, width, start=0, size=None):
        size = width if size is None else size
        return pl.ds(pl.multiple_of(core * width + start, WIDTH), size)

    def half(core):
        return pl.ds(pl.multiple_of(core * WIDTH, WIDTH), WIDTH)

    prompt = (pk_ref, pv_ref)

    local = [
        pltpu.make_async_copy(q_ref.at[:, cols(mine, 1024)], qin.at[0], loc_sem),
        pltpu.make_async_copy(og_ref.at[:, cols(mine, 1024)], oin.at[0], loc_sem),
        pltpu.make_async_copy(rk_ref.at[:, cols(mine, 256)], rkin.at[0], loc_sem),
        pltpu.make_async_copy(rv_ref.at[:, cols(mine, 256)], rvin.at[0], loc_sem),
    ]
    for t in range(2):
        for hh in range(HEADS):
            local.append(
                pltpu.make_async_copy(
                    prompt[t].at[:, cols(mine, 256, hh * WIDTH, WIDTH)],
                    kv.at[t, hh, 0, half(c)],
                    loc_sem,
                )
            )
    for copy in local:
        copy.start()

    barrier = pltpu.get_barrier_semaphore()
    for target in (*straight, *cross, mate):
        pl.semaphore_signal(barrier, inc=1, device_id={"grp": target}, device_id_type=MESH)
    pl.semaphore_wait(barrier, 5)

    def start(copy):
        copy.start()

    streams = ((KEY, UP), (VALUE, DOWN), (VALUE, UP), (KEY, DOWN))

    def first_hop(hh, which=streams):
        for t, d in which:
            for heads, target in ((mine, straight[d]), (theirs, cross[d])):
                start(
                    remote(
                        prompt[t].at[:, cols(heads, 256, hh * WIDTH, WIDTH)],
                        kv.at[t, hh, slot_of(d, 1), half(c)],
                        send_sem.at[0],
                        ag_recv.at[t, hh, d, 0],
                        target,
                    )
                )

    def pair(i, src, dst, send=2):
        start(remote(src, dst, send_sem.at[send], pair_recv.at[i], mate))

    def arrival(ref, sem):
        pltpu.make_async_copy(ref, ref, sem).wait()

    first_hop(0)
    pair(0, rk_ref.at[:, cols(theirs, 256)], rkin.at[1])
    pair(0, rv_ref.at[:, cols(theirs, 256)], rvin.at[1])
    pair(0, q_ref.at[:, cols(theirs, 1024)], qin.at[1])
    pair(0, og_ref.at[:, cols(theirs, 1024)], oin.at[1])
    for t in range(2):
        for hh in range(HEADS):
            pair(1, prompt[t].at[:, cols(theirs, 256, hh * WIDTH, WIDTH)], kv.at[t, hh, 0, half(c)])
    first_hop(1, streams[:2])

    for s in range(16):
        seen = mask_ref[0, order_ref[s]]
        row = jnp.full((1, LANES), seen, jnp.int32).astype(jnp.float32)
        meta[0, pl.ds(s, 1), :] = (1.0 - jnp.minimum(row, 1.0)) * HIDDEN
    meta[0, pl.ds(16, 8), :] = jnp.full((8, LANES), len_ref[0], jnp.int32).astype(jnp.float32)
    pair(2, meta.at[0], meta.at[1], send=3)

    arrival(kv.at[:, :, :3], loc_sem)
    arrival(kv.at[:, 0, :5], pair_recv.at[0])
    arrival(meta.at[1], pair_recv.at[2])

    for hh in range(HEADS):
        for p in range(2):
            for g in range(MEMBERS):
                rows = pl.ds(p * HALF + g * WIDTH, WIDTH)
                lanes = pl.ds((hh * MEMBERS + g) * WIDTH, WIDTH)
                qs[hh, rows, :] = qin[p, :, lanes]
                os_[hh, rows, :] = oin[p, :, lanes]

    def own_block(hh):
        for p in range(2):
            keys = rkin[p, :, pl.ds(hh * WIDTH, WIDTH)]
            values = rvin[p, :, pl.ds(hh * WIDTH, WIDTH)]

            for b in range(HALF // LANES):
                lanes = pl.ds(b * LANES, LANES)
                rows = pl.ds(p * HALF + b * LANES, LANES)
                s = dot_nt(keys, qs[hh, rows, :])
                dp = dot_nt(values, os_[hh, rows, :])
                key_at = lax.broadcasted_iota(jnp.int32, (WIDTH, LANES), 0)
                row_at = lax.broadcasted_iota(jnp.int32, (WIDTH, LANES), 1) % WIDTH
                s = jnp.where(key_at <= row_at, s * SCALE, HIDDEN)
                top = jnp.max(s, axis=0, keepdims=True)
                e = jnp.exp2(s - top)
                er_buf[hh, p, :, lanes] = e
                dr_buf[hh, p, :, lanes] = dp
                m_run[hh, :, rows] = top
                mr_save[hh, :, rows] = top
                l_run[hh, :, rows] = jnp.sum(e, axis=0, keepdims=True)
                w_run[hh, :, rows] = jnp.sum(e * dp, axis=0, keepdims=True)

    def tile_bias(p, slot, part):
        tile = ((z + RING - slot) % RING) * 2 + part
        return meta[p, pl.ds(tile, 1), :]

    def forward(hh, slot):
        for p in range(2):
            bias = [tile_bias(p, slot, part) for part in range(2)]

            for b in range(HALF // LANES):
                lanes = pl.ds(p * HALF + b * LANES, LANES)
                s = dot_nt(kv[KEY, hh, slot], qs[hh, lanes, :])
                dp = dot_nt(kv[VALUE, hh, slot], os_[hh, lanes, :])
                d_buf[hh, slot, :, lanes] = dp
                old = m_run[hh, :, lanes]
                top = old
                for part in range(2):
                    high = jnp.max(s[part * WIDTH : (part + 1) * WIDTH], axis=0, keepdims=True)
                    top = jnp.maximum(top, high * SCALE + bias[part])
                less = jnp.exp2(old - top)
                total = l_run[hh, :, lanes] * less
                weighted = w_run[hh, :, lanes] * less
                for part in range(2):
                    rows = slice(part * WIDTH, (part + 1) * WIDTH)
                    e = jnp.exp2(s[rows] * SCALE - (top - bias[part]))
                    e_buf[hh, slot, rows, lanes] = e
                    total = total + jnp.sum(e, axis=0, keepdims=True)
                    weighted = weighted + jnp.sum(e * dp[rows], axis=0, keepdims=True)
                m_run[hh, :, lanes] = top
                m_save[hh, slot, :, lanes] = top
                l_run[hh, :, lanes] = total
                w_run[hh, :, lanes] = weighted

    def gather(hh, hop, which=streams):
        for t, d in which:
            if hop > HOPS[t][d]:
                continue
            here = kv.at[t, hh, slot_of(d, hop)]
            arrival(here, ag_recv.at[t, hh, d, hop - 1])
            if hop < HOPS[t][d]:
                start(
                    remote(
                        here,
                        kv.at[t, hh, slot_of(d, hop + 1)],
                        send_sem.at[0],
                        ag_recv.at[t, hh, d, hop],
                        straight[d],
                    )
                )

    def settle(hh):
        for p in range(2):
            for b in range(HALF // LANES):
                lanes = pl.ds(p * HALF + b * LANES, LANES)
                total = l_run[hh, :, lanes]
                w_run[hh, :, lanes] = w_run[hh, :, lanes] / total
                at = (lax.broadcasted_iota(jnp.int32, (1, LANES), 1) % WIDTH).astype(jnp.float32)
                live = at < meta[p, pl.ds(16, 1), :]
                l_run[hh, :, lanes] = jnp.where(live, 1.0 / total, 0.0)

    def backward(hh, slot):
        keys = kv[KEY, hh, slot].T

        for b in range(ROWS // LANES):
            lanes = pl.ds(b * LANES, LANES)
            factor = jnp.exp2(m_save[hh, slot, :, lanes] - m_run[hh, :, lanes]) * l_run[hh, :, lanes]
            prob = e_buf[hh, slot, :, lanes] * factor
            p_tmp[:, lanes] = prob.astype(jnp.bfloat16)
            ds = (prob * (d_buf[hh, slot, :, lanes] - w_run[hh, :, lanes])).astype(jnp.bfloat16)
            ds_tmp[:, lanes] = ds
            turned = dot_nn(keys, ds)
            dq_t[hh, :, lanes] = turned if slot == 4 else dq_t[hh, :, lanes] + turned

        grad[KEY, hh, slot] = dot_nn(ds_tmp[...], qs[hh])
        grad[VALUE, hh, slot] = dot_nn(p_tmp[...], os_[hh])

    def pass_on(t, hh, d, hop, slot):
        i = hop - 1
        if hop == 1:
            sbuf[t, hh, d, i] = grad[t, hh, slot].astype(jnp.bfloat16)
        else:
            arrived = rbuf.at[t, hh, d, i - 1]
            arrival(arrived, rs_recv.at[t, hh, d, i - 1])
            sbuf[t, hh, d, i] = (grad[t, hh, slot] + arrived[...].astype(jnp.float32)).astype(jnp.bfloat16)
        if hop < HOPS[t][d]:
            start(
                remote(
                    sbuf.at[t, hh, d, i],
                    rbuf.at[t, hh, d, i],
                    send_sem.at[1],
                    rs_recv.at[t, hh, d, i],
                    straight[d],
                )
            )
        else:
            for way, (core, target) in enumerate(((c, straight[d]), (other, cross[d]))):
                start(
                    remote(
                        sbuf.at[t, hh, d, i, half(core)],
                        fin.at[t, hh, d, way],
                        send_sem.at[1],
                        rs_recv.at[t, hh, d, 3],
                        target,
                    )
                )

    def scatter(hh, away, first=None):
        for t, d in streams:
            hop = HOPS[t][d] - away + 1
            if hop > 0 and first in (None, hop == 1):
                pass_on(t, hh, d, hop, RING - away if d == UP else away)

    def own_chunk(hh):
        backward(hh, 0)
        for t in range(2):
            pair(3 + hh, grad.at[t, hh, 0, half(other)], mate_grad.at[hh, t])

    def own_tokens(hh):
        lanes = pl.ds(hh * WIDTH, WIDTH)
        for p in range(2):
            rows = pl.ds(p * HALF, HALF)
            factor = jnp.exp2(mr_save[hh, :, rows] - m_run[hh, :, rows]) * l_run[hh, :, rows]
            prob = er_buf[hh, p] * factor
            ds = (prob * (dr_buf[hh, p] - w_run[hh, :, rows])).astype(jnp.bfloat16)
            dq_t[hh, :, rows] += dot_tn(rkin[p, :, lanes], ds)
            key_part = dot_nn(ds, qs[hh, rows, :]) * ROOT
            value_part = dot_nn(prob.astype(jnp.bfloat16), os_[hh, rows, :])
            if p == 0:
                drk_out[:, cols(mine, 256, hh * WIDTH, WIDTH)] = key_part
                drv_out[:, cols(mine, 256, hh * WIDTH, WIDTH)] = value_part
            else:
                drk_stage[:, lanes] = key_part
                drv_stage[:, lanes] = value_part

    def give_own():
        for stage, out in ((drk_stage, drk_out), (drv_stage, drv_out)):
            pair(5, stage, out.at[:, cols(mine, 256)])

    def give_query(hh):
        for p in (1, 0):
            for g in range(MEMBERS):
                block = dq_t[hh, :, pl.ds(p * HALF + g * WIDTH, WIDTH)].T * ROOT
                if p == 0:
                    dq_out[:, cols(mine, 1024, (hh * MEMBERS + g) * WIDTH, WIDTH)] = block
                else:
                    dq_stage[:, pl.ds((hh * MEMBERS + g) * WIDTH, WIDTH)] = block
            if p == 1:
                pair(
                    5,
                    dq_stage.at[:, pl.ds(hh * HALF, HALF)],
                    dq_out.at[:, cols(mine, 1024, hh * HALF, HALF)],
                )

    result = (dpk_out, dpv_out)

    def finish(hh):
        arrival(mate_grad.at[hh], pair_recv.at[3 + hh])
        for t in range(2):
            for d in (UP, DOWN):
                arrival(fin.at[t, hh, d], rs_recv.at[t, hh, d, 3])
            for way, heads in enumerate((mine, theirs)):
                share = grad[t, hh, 0, half(c), :] if way == 0 else mate_grad[hh, t]
                for d in (UP, DOWN):
                    share = share + fin[t, hh, d, way].astype(jnp.float32)
                if t == KEY:
                    share = share * ROOT
                result[t][:, cols(heads, 256, hh * WIDTH, WIDTH)] = share

    own_block(0)
    own_block(1)
    arrival(kv.at[0, 0, :2], pair_recv.at[1])
    forward(0, 0)
    gather(0, 1)
    first_hop(1, streams[2:])
    forward(1, 0)
    forward(0, 1)
    forward(0, 7)
    gather(1, 1, streams[:2])
    gather(0, 2)
    gather(1, 1, streams[2:])
    forward(0, 2)
    forward(0, 6)
    forward(1, 1)
    forward(1, 7)
    gather(1, 2, streams[:2])
    gather(0, 3)
    gather(1, 2, streams[2:])
    forward(0, 3)
    forward(0, 5)
    forward(1, 2)
    forward(1, 6)
    gather(1, 3, streams[:2])
    gather(0, 4)
    forward(0, 4)
    settle(0)
    backward(0, 4)
    scatter(0, 4)
    gather(1, 3, streams[2:])
    backward(0, 5)
    backward(0, 3)
    scatter(0, 3, True)
    forward(1, 3)
    forward(1, 5)
    gather(1, 4)
    forward(1, 4)
    settle(1)
    backward(1, 4)
    scatter(1, 4)
    scatter(0, 3, False)
    backward(1, 5)
    backward(1, 3)
    scatter(1, 3, True)
    backward(0, 6)
    backward(0, 2)
    scatter(1, 3, False)
    scatter(0, 2)
    backward(1, 6)
    backward(1, 2)
    backward(0, 7)
    backward(0, 1)
    scatter(1, 2)
    scatter(0, 1)
    own_tokens(0)
    own_tokens(1)
    give_own()
    backward(1, 7)
    backward(1, 1)
    scatter(1, 1)
    own_chunk(0)
    own_chunk(1)
    give_query(0)
    give_query(1)
    finish(0)
    finish(1)

    arrival(kv.at[:, :, :3], pair_recv.at[5])
    for i in range(3):
        arrival(kv.at[:, :, :7], send_sem.at[i])
    arrival(meta.at[1], send_sem.at[3])


def deliver(*refs):
    given, out, sem = refs[:5], refs[5:10], refs[10]
    copies = [pltpu.make_async_copy(given[i], out[i], sem.at[i]) for i in range(5)]
    for copy in copies:
        copy.start()
    for copy in copies:
        copy.wait()


def local(*args):
    bf16, f32 = jnp.bfloat16, jnp.float32
    vmem = pltpu.VMEM
    dma = pltpu.SemaphoreType.DMA
    any_ = pl.BlockSpec(memory_space=pl.ANY)
    smem = pl.BlockSpec(memory_space=pltpu.SMEM)
    in_vmem = pl.BlockSpec(memory_space=pltpu.VMEM)
    shapes = [(WIDTH, 2048)] + [(WIDTH, 512)] * 4
    inside = pl.pallas_call(
        kernel,
        out_shape=[pltpu.VMEM(shape, f32) for shape in shapes],
        in_specs=[any_] * 6 + [smem] * 3,
        out_specs=[in_vmem] * 5,
        scratch_shapes=[
            vmem((2, WIDTH, 1024), bf16),
            vmem((2, WIDTH, 1024), bf16),
            vmem((2, WIDTH, 256), bf16),
            vmem((2, WIDTH, 256), bf16),
            vmem((2, 24, LANES), f32),
            vmem((HEADS, ROWS, WIDTH), bf16),
            vmem((HEADS, ROWS, WIDTH), bf16),
            vmem((2, HEADS, RING, CHUNK, WIDTH), bf16),
            vmem((HEADS, RING, CHUNK, ROWS), f32),
            vmem((HEADS, RING, CHUNK, ROWS), f32),
            vmem((HEADS, 2, WIDTH, HALF), f32),
            vmem((HEADS, 2, WIDTH, HALF), f32),
            vmem((HEADS, 1, ROWS), f32),
            vmem((HEADS, 1, ROWS), f32),
            vmem((HEADS, 1, ROWS), f32),
            vmem((HEADS, RING, 1, ROWS), f32),
            vmem((HEADS, 1, ROWS), f32),
            vmem((CHUNK, ROWS), bf16),
            vmem((CHUNK, ROWS), bf16),
            vmem((2, HEADS, RING, CHUNK, WIDTH), f32),
            vmem((2, HEADS, 2, 4, CHUNK, WIDTH), bf16),
            vmem((2, HEADS, 2, 3, CHUNK, WIDTH), bf16),
            vmem((2, HEADS, 2, 2, WIDTH, WIDTH), bf16),
            vmem((HEADS, 2, WIDTH, WIDTH), f32),
            vmem((HEADS, WIDTH, ROWS), f32),
            vmem((WIDTH, 1024), f32),
            vmem((WIDTH, 256), f32),
            vmem((WIDTH, 256), f32),
            pltpu.SemaphoreType.DMA,
            dma((4,)),
            dma((6,)),
            dma((2, HEADS, 2, 4)),
            dma((2, HEADS, 2, 4)),
        ],
        compiler_params=pltpu.CompilerParams(
            collective_id=0, has_side_effects=True, vmem_limit_bytes=54 * MIB
        ),
        name="tree_attention_backward",
    )(*args)
    return pl.pallas_call(
        deliver,
        out_shape=[jax.ShapeDtypeStruct(shape, f32) for shape in shapes],
        in_specs=[in_vmem] * 5,
        out_specs=[any_] * 5,
        scratch_shapes=[dma((5,))],
        compiler_params=pltpu.CompilerParams(vmem_limit_bytes=MIB),
        name="deliver",
    )(*inside)


def solution(mesh):
    rows = P(("dp", "grp"), "head")
    return jax.shard_map(
        local,
        mesh=mesh,
        in_specs=(rows,) * 6 + (P(("dp", "grp")), P(("dp", "grp"), None), P("dp")),
        out_specs=(rows,) * 5,
        check_vma=False,
    )
```

```python
import functools
import math

import jax
import jax.numpy as jnp
from jax import lax
from jax.experimental import pallas as pl
from jax.experimental.pallas import tpu as pltpu
from jax.sharding import PartitionSpec as P

MESH = pl.DeviceIdType.MESH
WIDTH = 128
RING = 8
HEADS = 2
MEMBERS = 4
HALF = MEMBERS * WIDTH
ROWS = 2 * HALF
CHUNK = 2 * WIDTH
LANES = 512
UP, DOWN = 0, 1
KEY, VALUE = 0, 1
HOPS = ((4, 3), (3, 4))
ROOT = 1.0 / math.sqrt(WIDTH)
SCALE = ROOT * math.log2(math.e)
HIDDEN = -1e30
MIB = 1024 * 1024


def dot_nt(a, b):
    return lax.dot_general(a, b, (((1,), (1,)), ((), ())), preferred_element_type=jnp.float32)


def dot_nn(a, b):
    return jnp.dot(a, b, preferred_element_type=jnp.float32)


def dot_tn(a, b):
    return lax.dot_general(a, b, (((0,), (0,)), ((), ())), preferred_element_type=jnp.float32)


def slot_of(direction, hop):
    return hop if direction == UP else RING - hop


def kernel(
    q_ref, og_ref, rk_ref, rv_ref, pk_ref, pv_ref, len_in, mask_in, order_in,
    dq_out, drk_out, drv_out, dpk_out, dpv_out,
    qin, oin, rkin, rvin, meta, qs, os_, kv,
    e_buf, d_buf, er_buf, dr_buf, m_run, l_run, w_run, m_save, mr_save,
    grad, sbuf, rbuf, fin, mate_grad, dq_t, dq_stage, drk_stage, drv_stage,
    len_ref, mask_ref, order_ref, loc_sem, small_sem, send_sem, pair_recv, ag_recv, rs_recv,
):
    me = lax.axis_index("grp")
    z, c = me // 2, me % 2
    other = 1 - c
    above, below = (z + 1) % RING, (z + RING - 1) % RING
    straight = (above * 2 + c, below * 2 + c)
    cross = (above * 2 + other, below * 2 + other)
    mate = z * 2 + other
    mine = c
    theirs = 1 - mine

    def remote(src, dst, send, recv, target):
        return pltpu.make_async_remote_copy(
            src_ref=src, dst_ref=dst, send_sem=send, recv_sem=recv,
            device_id={"grp": target}, device_id_type=MESH,
        )

    def cols(core, width, start=0, size=None):
        size = width if size is None else size
        return pl.ds(pl.multiple_of(core * width + start, WIDTH), size)

    def half(core):
        return pl.ds(pl.multiple_of(core * WIDTH, WIDTH), WIDTH)

    barrier = pltpu.get_barrier_semaphore()
    for target in (*straight, *cross, mate):
        pl.semaphore_signal(barrier, inc=1, device_id={"grp": target}, device_id_type=MESH)

    prompt = (pk_ref, pv_ref)

    local = [
        pltpu.make_async_copy(q_ref.at[:, cols(mine, 1024)], qin.at[0], loc_sem),
        pltpu.make_async_copy(og_ref.at[:, cols(mine, 1024)], oin.at[0], loc_sem),
        pltpu.make_async_copy(rk_ref.at[:, cols(mine, 256)], rkin.at[0], loc_sem),
        pltpu.make_async_copy(rv_ref.at[:, cols(mine, 256)], rvin.at[0], loc_sem),
    ]
    for t in range(2):
        for hh in range(HEADS):
            local.append(
                pltpu.make_async_copy(
                    prompt[t].at[:, cols(mine, 256, hh * WIDTH, WIDTH)],
                    kv.at[t, hh, 0, half(c)],
                    loc_sem,
                )
            )
    small = [
        pltpu.make_async_copy(src, dst, small_sem.at[i])
        for i, (src, dst) in enumerate(((len_in, len_ref), (mask_in, mask_ref), (order_in, order_ref)))
    ]
    for copy in local + small:
        copy.start()

    pl.semaphore_wait(barrier, 5)

    def start(copy):
        copy.start()

    streams = ((KEY, UP), (VALUE, DOWN), (VALUE, UP), (KEY, DOWN))

    def first_hop(hh, which=streams):
        for t, d in which:
            for heads, target in ((mine, straight[d]), (theirs, cross[d])):
                start(
                    remote(
                        prompt[t].at[:, cols(heads, 256, hh * WIDTH, WIDTH)],
                        kv.at[t, hh, slot_of(d, 1), half(c)],
                        send_sem.at[0],
                        ag_recv.at[t, hh, d, 0],
                        target,
                    )
                )

    def pair(i, src, dst, send=2):
        start(remote(src, dst, send_sem.at[send], pair_recv.at[i], mate))

    def arrival(ref, sem):
        pltpu.make_async_copy(ref, ref, sem).wait()

    first_hop(0)
    pair(0, rk_ref.at[:, cols(theirs, 256)], rkin.at[1])
    pair(0, rv_ref.at[:, cols(theirs, 256)], rvin.at[1])
    pair(0, q_ref.at[:, cols(theirs, 1024)], qin.at[1])
    pair(0, og_ref.at[:, cols(theirs, 1024)], oin.at[1])
    for t in range(2):
        for hh in range(HEADS):
            pair(1, prompt[t].at[:, cols(theirs, 256, hh * WIDTH, WIDTH)], kv.at[t, hh, 0, half(c)])
    first_hop(1, streams[:2])

    for copy in small:
        copy.wait()
    for s in range(16):
        seen = mask_ref[0, order_ref[s]]
        row = jnp.full((1, LANES), seen, jnp.int32).astype(jnp.float32)
        meta[0, pl.ds(s, 1), :] = (1.0 - jnp.minimum(row, 1.0)) * HIDDEN
    meta[0, pl.ds(16, 8), :] = jnp.full((8, LANES), len_ref[0], jnp.int32).astype(jnp.float32)
    pair(2, meta.at[0], meta.at[1], send=3)

    arrival(kv.at[:, :, :3], loc_sem)
    arrival(kv.at[:, 0, :5], pair_recv.at[0])
    arrival(meta.at[1], pair_recv.at[2])

    for hh in range(HEADS):
        for p in range(2):
            for g in range(MEMBERS):
                rows = pl.ds(p * HALF + g * WIDTH, WIDTH)
                lanes = pl.ds((hh * MEMBERS + g) * WIDTH, WIDTH)
                qs[hh, rows, :] = qin[p, :, lanes]
                os_[hh, rows, :] = oin[p, :, lanes]

    def own_block(hh):
        for p in range(2):
            keys = rkin[p, :, pl.ds(hh * WIDTH, WIDTH)]
            values = rvin[p, :, pl.ds(hh * WIDTH, WIDTH)]

            for b in range(HALF // LANES):
                lanes = pl.ds(b * LANES, LANES)
                rows = pl.ds(p * HALF + b * LANES, LANES)
                s = dot_nt(keys, qs[hh, rows, :])
                dp = dot_nt(values, os_[hh, rows, :])
                key_at = lax.broadcasted_iota(jnp.int32, (WIDTH, LANES), 0)
                row_at = lax.broadcasted_iota(jnp.int32, (WIDTH, LANES), 1) % WIDTH
                s = jnp.where(key_at <= row_at, s * SCALE, HIDDEN)
                top = jnp.max(s, axis=0, keepdims=True)
                e = jnp.exp2(s - top)
                er_buf[hh, p, :, lanes] = e
                dr_buf[hh, p, :, lanes] = dp
                m_run[hh, :, rows] = top
                mr_save[hh, :, rows] = top
                l_run[hh, :, rows] = jnp.sum(e, axis=0, keepdims=True)
                w_run[hh, :, rows] = jnp.sum(e * dp, axis=0, keepdims=True)

    def tile_bias(p, slot, part):
        tile = ((z + RING - slot) % RING) * 2 + part
        return meta[p, pl.ds(tile, 1), :]

    def rows_of(kind, hh, slots):
        return jnp.concatenate([kv[kind, hh, slot] for slot in slots], axis=0)

    def forward(hh, *slots):
        tiles = [(n, slot, part) for n, slot in enumerate(slots) for part in range(2)]
        for p in range(2):
            lanes = pl.ds(p * HALF, HALF)
            s = dot_nt(rows_of(KEY, hh, slots), qs[hh, lanes, :])
            dp = dot_nt(rows_of(VALUE, hh, slots), os_[hh, lanes, :])
            for n, slot in enumerate(slots):
                d_buf[hh, slot, :, lanes] = dp[n * CHUNK : (n + 1) * CHUNK]
            old = m_run[hh, :, lanes]
            top = old
            for n, slot, part in tiles:
                rows = slice(n * CHUNK + part * WIDTH, n * CHUNK + (part + 1) * WIDTH)
                high = jnp.max(s[rows], axis=0, keepdims=True)
                top = jnp.maximum(top, high * SCALE + tile_bias(p, slot, part))
            less = jnp.exp2(old - top)
            total = l_run[hh, :, lanes] * less
            weighted = w_run[hh, :, lanes] * less
            for n, slot, part in tiles:
                rows = slice(n * CHUNK + part * WIDTH, n * CHUNK + (part + 1) * WIDTH)
                e = jnp.exp2(s[rows] * SCALE - (top - tile_bias(p, slot, part)))
                e_buf[hh, slot, pl.ds(part * WIDTH, WIDTH), lanes] = e
                total = total + jnp.sum(e, axis=0, keepdims=True)
                weighted = weighted + jnp.sum(e * dp[rows], axis=0, keepdims=True)
            m_run[hh, :, lanes] = top
            for slot in slots:
                m_save[hh, slot, :, lanes] = top
            l_run[hh, :, lanes] = total
            w_run[hh, :, lanes] = weighted

    def gather(hh, hop, which=streams):
        for t, d in which:
            if hop > HOPS[t][d]:
                continue
            here = kv.at[t, hh, slot_of(d, hop)]
            arrival(here, ag_recv.at[t, hh, d, hop - 1])
            if hop < HOPS[t][d]:
                start(
                    remote(
                        here,
                        kv.at[t, hh, slot_of(d, hop + 1)],
                        send_sem.at[0],
                        ag_recv.at[t, hh, d, hop],
                        straight[d],
                    )
                )

    def settle(hh):
        for p in range(2):
            for b in range(HALF // LANES):
                lanes = pl.ds(p * HALF + b * LANES, LANES)
                total = l_run[hh, :, lanes]
                w_run[hh, :, lanes] = w_run[hh, :, lanes] / total
                at = (lax.broadcasted_iota(jnp.int32, (1, LANES), 1) % WIDTH).astype(jnp.float32)
                live = at < meta[p, pl.ds(16, 1), :]
                l_run[hh, :, lanes] = jnp.where(live, 1.0 / total, 0.0)

    def backward(hh, *slots):
        keys = rows_of(KEY, hh, slots).T
        for p in range(2):
            lanes = pl.ds(p * HALF, HALF)
            probs, scores = [], []
            for slot in slots:
                factor = jnp.exp2(m_save[hh, slot, :, lanes] - m_run[hh, :, lanes]) * l_run[hh, :, lanes]
                prob = e_buf[hh, slot, :, lanes] * factor
                probs.append(prob.astype(jnp.bfloat16))
                ds = prob * (d_buf[hh, slot, :, lanes] - w_run[hh, :, lanes])
                scores.append(ds.astype(jnp.bfloat16))
            ds = jnp.concatenate(scores, axis=0)
            parts = (dot_nn(ds, qs[hh, lanes, :]), dot_nn(jnp.concatenate(probs, axis=0), os_[hh, lanes, :]))
            for t in (KEY, VALUE):
                for n, slot in enumerate(slots):
                    part = parts[t][n * CHUNK : (n + 1) * CHUNK]
                    grad[t, hh, slot] = part if p == 0 else grad[t, hh, slot] + part
            turned = dot_nn(keys, ds)
            dq_t[hh, :, lanes] = turned if slots[0] == 4 else dq_t[hh, :, lanes] + turned

    def pass_on(t, hh, d, hop, slot):
        i = hop - 1
        if hop == 1:
            sbuf[t, hh, d, i] = grad[t, hh, slot].astype(jnp.bfloat16)
        else:
            arrived = rbuf.at[t, hh, d, i - 1]
            arrival(arrived, rs_recv.at[t, hh, d, i - 1])
            sbuf[t, hh, d, i] = (grad[t, hh, slot] + arrived[...].astype(jnp.float32)).astype(jnp.bfloat16)
        if hop < HOPS[t][d]:
            start(
                remote(
                    sbuf.at[t, hh, d, i],
                    rbuf.at[t, hh, d, i],
                    send_sem.at[1],
                    rs_recv.at[t, hh, d, i],
                    straight[d],
                )
            )
        else:
            for way, (core, target) in enumerate(((c, straight[d]), (other, cross[d]))):
                start(
                    remote(
                        sbuf.at[t, hh, d, i, half(core)],
                        fin.at[t, hh, d, way],
                        send_sem.at[1],
                        rs_recv.at[t, hh, d, 3],
                        target,
                    )
                )

    def scatter(hh, away, first=None):
        for t, d in streams:
            hop = HOPS[t][d] - away + 1
            if hop > 0 and first in (None, hop == 1):
                pass_on(t, hh, d, hop, RING - away if d == UP else away)

    def own_chunk(hh):
        backward(hh, 0)
        for t in range(2):
            pair(3 + hh, grad.at[t, hh, 0, half(other)], mate_grad.at[hh, t])

    def own_tokens(hh):
        lanes = pl.ds(hh * WIDTH, WIDTH)
        for p in range(2):
            rows = pl.ds(p * HALF, HALF)
            factor = jnp.exp2(mr_save[hh, :, rows] - m_run[hh, :, rows]) * l_run[hh, :, rows]
            prob = er_buf[hh, p] * factor
            ds = (prob * (dr_buf[hh, p] - w_run[hh, :, rows])).astype(jnp.bfloat16)
            dq_t[hh, :, rows] += dot_tn(rkin[p, :, lanes], ds)
            key_part = dot_nn(ds, qs[hh, rows, :]) * ROOT
            value_part = dot_nn(prob.astype(jnp.bfloat16), os_[hh, rows, :])
            if p == 0:
                drk_out[:, cols(mine, 256, hh * WIDTH, WIDTH)] = key_part
                drv_out[:, cols(mine, 256, hh * WIDTH, WIDTH)] = value_part
            else:
                drk_stage[:, lanes] = key_part
                drv_stage[:, lanes] = value_part

    def give_own():
        for stage, out in ((drk_stage, drk_out), (drv_stage, drv_out)):
            pair(5, stage, out.at[:, cols(mine, 256)])

    def give_query(hh):
        for p in (1, 0):
            for g in range(MEMBERS):
                block = dq_t[hh, :, pl.ds(p * HALF + g * WIDTH, WIDTH)].T * ROOT
                if p == 0:
                    dq_out[:, cols(mine, 1024, (hh * MEMBERS + g) * WIDTH, WIDTH)] = block
                else:
                    dq_stage[:, pl.ds((hh * MEMBERS + g) * WIDTH, WIDTH)] = block
            if p == 1:
                pair(
                    5,
                    dq_stage.at[:, pl.ds(hh * HALF, HALF)],
                    dq_out.at[:, cols(mine, 1024, hh * HALF, HALF)],
                )

    result = (dpk_out, dpv_out)

    def finish(hh):
        arrival(mate_grad.at[hh], pair_recv.at[3 + hh])
        for t in range(2):
            for d in (UP, DOWN):
                arrival(fin.at[t, hh, d], rs_recv.at[t, hh, d, 3])
            for way, heads in enumerate((mine, theirs)):
                share = grad[t, hh, 0, half(c), :] if way == 0 else mate_grad[hh, t]
                for d in (UP, DOWN):
                    share = share + fin[t, hh, d, way].astype(jnp.float32)
                if t == KEY:
                    share = share * ROOT
                result[t][:, cols(heads, 256, hh * WIDTH, WIDTH)] = share

    own_block(0)
    own_block(1)
    arrival(kv.at[0, 0, :2], pair_recv.at[1])
    forward(0, 0)
    gather(0, 1)
    first_hop(1, streams[2:])
    forward(1, 0)
    forward(0, 1, 7)
    gather(1, 1, streams[:2])
    gather(0, 2)
    gather(1, 1, streams[2:])
    forward(0, 2, 6)
    forward(1, 1, 7)
    gather(1, 2, streams[:2])
    gather(0, 3)
    gather(1, 2, streams[2:])
    forward(0, 3, 5)
    forward(1, 2, 6)
    gather(1, 3, streams[:2])
    gather(0, 4)
    forward(0, 4)
    settle(0)
    backward(0, 4)
    scatter(0, 4)
    gather(1, 3, streams[2:])
    backward(0, 5, 3)
    scatter(0, 3, True)
    forward(1, 3, 5)
    gather(1, 4)
    forward(1, 4)
    settle(1)
    backward(1, 4)
    scatter(1, 4)
    scatter(0, 3, False)
    backward(1, 5, 3)
    scatter(1, 3, True)
    backward(0, 6, 2)
    scatter(1, 3, False)
    scatter(0, 2)
    backward(1, 6, 2)
    backward(0, 7, 1)
    scatter(1, 2)
    scatter(0, 1)
    own_tokens(0)
    own_tokens(1)
    give_own()
    backward(1, 7, 1)
    scatter(1, 1)
    own_chunk(0)
    own_chunk(1)
    give_query(0)
    give_query(1)
    finish(0)
    finish(1)

    arrival(kv.at[:, :, :3], pair_recv.at[5])
    for i in range(3):
        arrival(kv.at[:, :, :7], send_sem.at[i])
    arrival(meta.at[1], send_sem.at[3])


def deliver(*refs):
    given, out, sem = refs[:5], refs[5:10], refs[10]
    copies = [pltpu.make_async_copy(given[i], out[i], sem.at[i]) for i in range(5)]
    for copy in copies:
        copy.start()
    for copy in copies:
        copy.wait()


def local(*args):
    bf16, f32 = jnp.bfloat16, jnp.float32
    vmem = pltpu.VMEM
    dma = pltpu.SemaphoreType.DMA
    any_ = pl.BlockSpec(memory_space=pl.ANY)
    in_vmem = pl.BlockSpec(memory_space=pltpu.VMEM)
    shapes = [(WIDTH, 2048)] + [(WIDTH, 512)] * 4
    inside = pl.pallas_call(
        kernel,
        out_shape=[pltpu.VMEM(shape, f32) for shape in shapes],
        in_specs=[any_] * 9,
        out_specs=[in_vmem] * 5,
        scratch_shapes=[
            vmem((2, WIDTH, 1024), bf16),
            vmem((2, WIDTH, 1024), bf16),
            vmem((2, WIDTH, 256), bf16),
            vmem((2, WIDTH, 256), bf16),
            vmem((2, 24, LANES), f32),
            vmem((HEADS, ROWS, WIDTH), bf16),
            vmem((HEADS, ROWS, WIDTH), bf16),
            vmem((2, HEADS, RING, CHUNK, WIDTH), bf16),
            vmem((HEADS, RING, CHUNK, ROWS), f32),
            vmem((HEADS, RING, CHUNK, ROWS), f32),
            vmem((HEADS, 2, WIDTH, HALF), f32),
            vmem((HEADS, 2, WIDTH, HALF), f32),
            vmem((HEADS, 1, ROWS), f32),
            vmem((HEADS, 1, ROWS), f32),
            vmem((HEADS, 1, ROWS), f32),
            vmem((HEADS, RING, 1, ROWS), f32),
            vmem((HEADS, 1, ROWS), f32),
            vmem((2, HEADS, RING, CHUNK, WIDTH), f32),
            vmem((2, HEADS, 2, 4, CHUNK, WIDTH), bf16),
            vmem((2, HEADS, 2, 3, CHUNK, WIDTH), bf16),
            vmem((2, HEADS, 2, 2, WIDTH, WIDTH), bf16),
            vmem((HEADS, 2, WIDTH, WIDTH), f32),
            vmem((HEADS, WIDTH, ROWS), f32),
            vmem((WIDTH, 1024), f32),
            vmem((WIDTH, 256), f32),
            vmem((WIDTH, 256), f32),
            pltpu.SMEM((1,), jnp.int32),
            pltpu.SMEM((1, 16), jnp.int32),
            pltpu.SMEM((16,), jnp.int32),
            pltpu.SemaphoreType.DMA,
            dma((3,)),
            dma((4,)),
            dma((6,)),
            dma((2, HEADS, 2, 4)),
            dma((2, HEADS, 2, 4)),
        ],
        compiler_params=pltpu.CompilerParams(
            collective_id=0, has_side_effects=True, vmem_limit_bytes=54 * MIB
        ),
        name="tree_attention_backward",
    )(*args)
    return pl.pallas_call(
        deliver,
        out_shape=[jax.ShapeDtypeStruct(shape, f32) for shape in shapes],
        in_specs=[in_vmem] * 5,
        out_specs=[any_] * 5,
        scratch_shapes=[dma((5,))],
        compiler_params=pltpu.CompilerParams(vmem_limit_bytes=MIB),
        name="deliver",
    )(*inside)


def solution(mesh):
    rows = P(("dp", "grp"), "head")
    return jax.shard_map(
        local,
        mesh=mesh,
        in_specs=(rows,) * 6 + (P(("dp", "grp")), P(("dp", "grp"), None), P("dp")),
        out_specs=(rows,) * 5,
        check_vma=False,
    )
```
